128 devices in a mesh: dp: 16 (over y, z_lo, core), seq: 8 (over x, z_hi).
Axes of the slice: x: 4, y: 4, z: 4 (z_hi: 2, z_lo: 2; z = z_hi * 2 + z_lo), core: 2. Of those that a mesh axis runs over, the one named last changes fastest.
Arguments:
- hidden_states: bfloat16 [16384, 5120], P(('dp', 'seq')), may hold values from -24 to 24
- value_weight: bfloat16 [5120, 1024], P('dp'), may hold values from -0.078125 to 0.078125
- query_states: bfloat16 [16384, 8192], P(('dp', 'seq')), may hold values from -140 to 140
- key_states: bfloat16 [16384, 1024], P(('dp', 'seq')), may hold values from -4.5 to 4.5
- cotangent: bfloat16 [16384, 8192], P(('dp', 'seq')), may hold values from -6 to 6
- lengths: int32 [16, 8], P('dp'), may hold values from 1 to 512, 1024 in all within a row
Outputs:
- attention_out: bfloat16 [16384, 8192], P(('dp', 'seq'))
- query_grad: bfloat16 [16384, 8192], P(('dp', 'seq'))
- key_grad: bfloat16 [16384, 1024], P(('dp', 'seq'))
- input_grad: bfloat16 [16384, 5120], P(('dp', 'seq'))
- value_weight_grad: float32 [5120, 1024], P('dp')
The draws below stay inside these ranges and needn't reach their ends.
Inputs may be any that keep to these rules, and one draw needn't show every extreme that they name: Row g lists the 8 response lengths of group g's pack; they sum to 1024 and the longest is 512.
All inputs are finite; a program needn't handle non-finite values.
Results may differ from the reference program's by a relative error of at most 0.04.
Values may be sent and summed in bfloat16 or wider, within the bound.
No kernel may reach another device: no remote copies, remote signals or barrier semaphores. Data moves between devices by JAX's collectives and lax.ppermute only.
A program may use at most 256 MiB of HBM per device.

```python
import math
import jax
import jax.numpy as jnp
import numpy as np
from jax import lax

D = 5120
HEADS = 64
KV_HEADS = 8
HEAD_DIM = 128
DOCS = 8
PACK = 1024
MOST = 512
TOKENS = 16384
N_DP = 16


def shared_keys(key):
    return jnp.clip(jax.random.normal(key, (TOKENS, KV_HEADS * HEAD_DIM), jnp.float32), -4.0, 4.0)


def draw_key_states(key, part):
    base = shared_keys(key)
    return base.astype(jnp.bfloat16)


def draw_query_states(key, part):
    key = jax.random.fold_in(key, 7)
    first_key = jax.random.fold_in(key, 0)
    drawn = jnp.clip(jax.random.normal(first_key, (TOKENS, HEADS * HEAD_DIM), jnp.float32), -4.0, 4.0)
    return drawn.astype(jnp.bfloat16)


def raised(drawn, key, source, target, blocks, factor):
    def block_of(dim):
        return (jnp.arange(drawn.shape[dim]) // (drawn.shape[dim] // blocks)).reshape((-1,) + (1,) * (drawn.ndim - 1 - dim))

    near = jax.random.permutation(key, blocks)[block_of(target)]
    other_side = (block_of(target) + blocks // 2) % blocks
    return jnp.where((block_of(source) == near) | (block_of(source) == other_side), factor * drawn, drawn)


def block_levels(own_key, extent, cuts, smallest, largest):
    def one(dim, shards_of):
        steps = jax.random.uniform(jax.random.fold_in(jax.random.fold_in(own_key, 6), dim), (shards_of,), jnp.float32, smallest / len(cuts), largest / len(cuts))
        return jnp.repeat(jnp.exp(steps), extent[dim] // shards_of).reshape((-1,) + (1,) * (len(extent) - dim - 1))

    gain = one(*cuts[0])
    for cut in cuts[1:]:
        gain = gain * one(*cut)
    return gain


def profile(number_of, total, most, skew):
    portions = [(1 << 20) // math.isqrt(standing ** skew) + 1 for standing in range(2, number_of + 1)]
    spare, counts = total - most - (number_of - 1), [1] * (number_of - 1)
    while spare > 0:
        movable = [i for i in range(number_of - 1) if counts[i] < most]
        whole, left = sum([portions[i] for i in movable]), spare
        for i in movable:
            more = min(most - counts[i], max(1, left * portions[i] // whole), spare)
            counts[i] = counts[i] + more
            spare = spare - more
    return np.array([most] + counts)


def ragged_sizes(stream_key, number_of, total, bound, skew):
    if number_of == 2:
        one = jax.random.randint(stream_key, (), max(1, total - bound), min(bound, total - 1) + 1)
        return jnp.stack([one, total - one])
    tallies = jnp.asarray(profile(number_of, total, bound, skew), jnp.int32)
    couples = (number_of - 1) // 2
    source_of, taker = tallies[1:1 + 2 * couples:2], tallies[2:2 + 2 * couples:2]
    margin = jnp.minimum(source_of - 1, bound - taker)
    passed = jax.random.randint(jax.random.fold_in(stream_key, 1), (couples,), 0, 1 << 20) % (margin + 1)
    tallies = tallies.at[1:1 + 2 * couples:2].set(source_of - passed).at[2:2 + 2 * couples:2].set(taker + passed)
    return tallies[jax.random.permutation(jax.random.fold_in(stream_key, 2), number_of)]


def gaussian(rng, dims, width, reach, cuts=(), kind=jnp.bfloat16):
    level = block_levels(rng, dims, cuts, -0.22, 0.18) if cuts else 1.0
    values = jax.random.normal(rng, dims, jnp.float32) * width * level
    return jnp.minimum(jnp.maximum(values, -reach), reach).astype(kind)


def heavy_noise(rng, dims, spread, bound, cuts, heavy, kind=jnp.bfloat16):
    drawn = spread * jax.random.normal(rng, dims, jnp.float32)
    if cuts:
        drawn = drawn * block_levels(rng, dims, cuts, -0.22, 0.18)
    return jnp.clip(raised(drawn, jax.random.fold_in(rng, 3), *heavy), -bound, bound).astype(kind)


def setup_inputs(seed: int = 0) -> dict:
    arg_keys = jax.random.split(jax.random.key(seed), 7)
    return {
        "hidden_states": heavy_noise(arg_keys[0], (TOKENS, D), 1.0, 24.0, ((0, 128),), (0, 1, 128, 5.5)),
        "value_weight": gaussian(arg_keys[1], (D, KV_HEADS * HEAD_DIM), D ** -0.5, 0.078125, ((0, 16),)),
        "query_states": draw_query_states(jax.random.fold_in(arg_keys[6], 71), 0),
        "key_states": draw_key_states(jax.random.fold_in(arg_keys[6], 71), 0),
        "cotangent": gaussian(arg_keys[4], (TOKENS, HEADS * HEAD_DIM), 1.0, 6.0, ((0, 128),)),
        "lengths": jax.vmap(lambda own: ragged_sizes(own, DOCS, PACK, MOST, 2))(jax.random.split(arg_keys[5], N_DP)).reshape((N_DP, DOCS)).astype(jnp.int32),
    }


def document_ids(lengths_row, positions):
    doc_ends = jnp.cumsum(lengths_row)
    return jnp.sum((positions[:, None] >= doc_ends[None, :-1]).astype(jnp.int32), axis=1)


def kv_group(operands):
    queries, keys_head, values_head, cot_head, lengths_row = operands
    positions = jnp.arange(PACK, dtype=jnp.int32)
    doc_ids = document_ids(lengths_row, positions)
    allowed = (doc_ids[:, None] == doc_ids[None, :]) & (positions[None, :] <= positions[:, None])
    score_scale = HEAD_DIM ** -0.5
    query_wide = queries.astype(jnp.float32)
    key_wide = keys_head.astype(jnp.float32)
    value_wide = values_head.astype(jnp.float32)
    cot_wide = cot_head.astype(jnp.float32)
    scores = jnp.einsum("qgd,kd->gqk", query_wide, key_wide) * score_scale
    scores = jnp.where(allowed[None], scores, -jnp.inf)
    highest = jnp.max(scores, axis=-1, keepdims=True)
    expo = jnp.exp(scores - highest)
    probabilities = expo / jnp.sum(expo, axis=-1, keepdims=True)
    rounded = lax.optimization_barrier(probabilities.astype(jnp.bfloat16)).astype(jnp.float32)
    attended = jnp.einsum("gqk,kd->qgd", rounded, value_wide).astype(jnp.bfloat16)
    attended = lax.optimization_barrier(attended)
    through_values = jnp.einsum("qgd,kd->gqk", cot_wide, value_wide)
    row_delta = jnp.einsum("qgd,qgd->gq", cot_wide, attended.astype(jnp.float32))
    score_grad = probabilities * (through_values - row_delta[:, :, None])
    score_grad = lax.optimization_barrier(score_grad.astype(jnp.bfloat16)).astype(jnp.float32)
    query_grad = (jnp.einsum("gqk,kd->qgd", score_grad, key_wide) * score_scale).astype(jnp.bfloat16)
    key_grad = (jnp.einsum("gqk,qgd->kd", score_grad, query_wide) * score_scale).astype(jnp.bfloat16)
    value_grad = jnp.einsum("gqk,qgd->kd", rounded, cot_wide).astype(jnp.bfloat16)
    return attended, query_grad, key_grad, value_grad


def reference(hidden_states, value_weight, query_states, key_states, cotangent, lengths):
    values = jnp.dot(hidden_states, value_weight, preferred_element_type=jnp.float32).astype(jnp.bfloat16)
    values = lax.optimization_barrier(values)
    group = HEADS // KV_HEADS

    def split_queries(table):
        shaped = table.reshape(N_DP, PACK, KV_HEADS, group, HEAD_DIM).transpose(0, 2, 1, 3, 4)
        return shaped.reshape(N_DP * KV_HEADS, PACK, group, HEAD_DIM)

    def split_keys(table):
        shaped = table.reshape(N_DP, PACK, KV_HEADS, HEAD_DIM).transpose(0, 2, 1, 3)
        return shaped.reshape(N_DP * KV_HEADS, PACK, HEAD_DIM)

    def join_queries(table):
        shaped = table.reshape(N_DP, KV_HEADS, PACK, group, HEAD_DIM).transpose(0, 2, 1, 3, 4)
        return shaped.reshape(TOKENS, HEADS * HEAD_DIM)

    def join_keys(table):
        shaped = table.reshape(N_DP, KV_HEADS, PACK, HEAD_DIM).transpose(0, 2, 1, 3)
        return shaped.reshape(TOKENS, KV_HEADS * HEAD_DIM)

    group_lengths = jnp.repeat(lengths, KV_HEADS, axis=0)
    attended, query_grad, key_grad, value_grad = lax.map(
        kv_group,
        (split_queries(query_states), split_keys(key_states), split_keys(values), split_queries(cotangent), group_lengths),
    )
    attention_out = join_queries(attended)
    query_out = join_queries(query_grad)
    key_out = join_keys(key_grad)
    value_rows = join_keys(value_grad)
    input_grad = jnp.dot(value_rows, value_weight.T, preferred_element_type=jnp.float32).astype(jnp.bfloat16)
    weight_grad = jnp.dot(hidden_states.T, value_rows, preferred_element_type=jnp.float32)
    return attention_out, query_out, key_out, input_grad, weight_grad
```

```python
import functools
import math

import jax
import jax.numpy as jnp
from jax import lax
from jax.experimental import pallas as pl
from jax.experimental.pallas import tpu as pltpu
from jax.sharding import PartitionSpec as P

HD = 128
KV = 8
G = 8
CH = 5
SC = HD**-0.5
L2 = SC * math.log2(math.e)
bf = jnp.bfloat16
f32 = jnp.float32
VL = 56 * 1024 * 1024

def probs_kernel(meta, q, do, k0,k1,k2,k3,k4, e_out, qt_out, dot_out, li_out, v0,v1,v2,v3,v4, bias):
    rows=q.shape[0]
    @pl.when(pl.program_id(0)==0)
    def _():
        s=meta[KV]
        r=lax.broadcasted_iota(jnp.int32,(1,rows),1)
        pos=r+s*rows
        start=jnp.zeros((1,rows),jnp.int32)
        total=meta[0]
        for d in range(1,8):
            start=jnp.where(pos>=total,total,start)
            total=total+meta[d]
        low=start-(s-(CH-1))*rows
        j=lax.broadcasted_iota(jnp.int32,(CH*rows,rows),0)
        ok=(j>=low)&(j<=r+(CH-1)*rows)
        bias[...]=jnp.where(ok,0.0,-1e30)
    for h in range(G):
        qt_out[0,:,h*rows:(h+1)*rows]=q[:,h*HD:(h+1)*HD].T
    ks=(k0,k1,k2,k3,k4)
    W=2
    n=W*rows
    for p in range(G//W):
        cols=slice(p*n,(p+1)*n)
        qt=qt_out[0,:,cols]
        ts=[]
        for c in range(CH):
            b=bias[c*rows:(c+1)*rows,:]
            b=jnp.concatenate([b]*W,axis=1)
            ts.append(jnp.dot(ks[c][...],qt,preferred_element_type=f32)*L2+b)
        m=functools.reduce(jnp.maximum,[jnp.max(t,axis=0,keepdims=True) for t in ts])
        l=jnp.zeros((1,n),f32)
        for c in range(CH):
            e=jnp.exp2(ts[c]-m)
            l=l+jnp.sum(e,axis=0,keepdims=True)
            e_out[0,c*rows:(c+1)*rows,cols]=e.astype(bf)
        li=1.0/l
        li_out[0,:,cols]=jnp.broadcast_to(li,(8,n))
        dt=jnp.concatenate([do[:,h*HD:(h+1)*HD].T for h in range(p*W,(p+1)*W)],axis=1)
        dot_out[0,:,cols]=(dt.astype(f32)*li).astype(bf)
    dall=dot_out[0]
    for c,v in enumerate((v0,v1,v2,v3,v4)):
        v[...]=lax.dot_general(e_out[0,c*rows:(c+1)*rows,:],dall,(((1,),(1,)),((),())),preferred_element_type=f32).astype(v.dtype)

def probs_call(meta,q,do,ks):
    rows=q.shape[0]
    wide=G*rows
    bs=lambda: pl.BlockSpec((rows,HD),lambda j:(0,j))
    bw=lambda: pl.BlockSpec((rows,G*HD),lambda j:(0,j))
    b3=lambda a,b: pl.BlockSpec((1,a,b),lambda j:(j,0,0))
    S=jax.ShapeDtypeStruct
    return pl.pallas_call(probs_kernel,grid=(KV,),
        in_specs=[pl.BlockSpec(memory_space=pltpu.SMEM),bw(),bw()]+[bs() for _ in range(CH)],
        out_specs=[b3(CH*rows,wide),b3(HD,wide),b3(HD,wide),b3(8,wide)]+[bs() for _ in range(CH)],
        out_shape=[S((KV,CH*rows,wide),bf),S((KV,HD,wide),bf),S((KV,HD,wide),bf),S((KV,8,wide),f32)]+[S((rows,KV*HD),bf)]*(CH-1)+[S((rows,KV*HD),f32)],
        scratch_shapes=[pltpu.VMEM((CH*rows,rows),f32)],
        compiler_params=pltpu.CompilerParams(vmem_limit_bytes=VL),
        cost_estimate=pl.CostEstimate(flops=2*2*KV*CH*rows*wide*HD,bytes_accessed=KV*CH*rows*wide*2+8*rows*8192,transcendentals=KV*CH*rows*wide),
        )(meta,q,do,*ks)

def grads_kernel(e,qt,dott,li,k0,k1,k2,k3,k4,v0,v1,v2,v3,v4,out,dq,g0,g1,g2,g3,g4,ds):
    rows=out.shape[0]
    ks=(k0,k1,k2,k3,k4); vs=(v0,v1,v2,v3,v4)
    W=2; n=W*rows
    kt=jnp.concatenate([k[...].T for k in ks],axis=1)
    vt=jnp.concatenate([v[...].T for v in vs],axis=1)
    for p in range(G//W):
        cols=slice(p*n,(p+1)*n)
        o=jnp.dot(vt,e[0,:,cols],preferred_element_type=f32)*li[0,0:1,cols]
        ob=o.astype(bf)
        dt=dott[0,:,cols]
        delta=jnp.sum(dt.astype(f32)*o,axis=0,keepdims=True)
        for c in range(CH):
            dp=jnp.dot(vs[c][...],dt,preferred_element_type=f32)
            ds[c*rows:(c+1)*rows,cols]=(e[0,c*rows:(c+1)*rows,cols].astype(f32)*(dp-delta)).astype(bf)
        dqt=(jnp.dot(kt,ds[:,cols],preferred_element_type=f32)*SC).astype(bf)
        for w in range(W):
            h=p*W+w
            out[:,h*HD:(h+1)*HD]=ob[:,w*rows:(w+1)*rows].T
            dq[:,h*HD:(h+1)*HD]=dqt[:,w*rows:(w+1)*rows].T
    qall=qt[0]
    for c,g in enumerate((g0,g1,g2,g3,g4)):
        g[...]=(lax.dot_general(ds[c*rows:(c+1)*rows,:],qall,(((1,),(1,)),((),())),preferred_element_type=f32)*SC).astype(g.dtype)

def grads_call(e,qt,dott,li,ks,vs):
    rows=ks[0].shape[0]; wide=G*rows
    bs=lambda: pl.BlockSpec((rows,HD),lambda j:(0,j))
    bw=lambda: pl.BlockSpec((rows,G*HD),lambda j:(0,j))
    b3=lambda a,b: pl.BlockSpec((1,a,b),lambda j:(j,0,0))
    S=jax.ShapeDtypeStruct
    return pl.pallas_call(grads_kernel,grid=(KV,),
        in_specs=[b3(CH*rows,wide),b3(HD,wide),b3(HD,wide),b3(8,wide)]+[bs() for _ in range(2*CH)],
        out_specs=[bw(),bw()]+[bs() for _ in range(CH)],
        out_shape=[S((rows,KV*G*HD),bf)]*2+[S((rows,KV*HD),bf)]*(CH-1)+[S((rows,KV*HD),f32)],
        scratch_shapes=[pltpu.VMEM((CH*rows,wide),bf)],
        compiler_params=pltpu.CompilerParams(vmem_limit_bytes=VL),
        cost_estimate=pl.CostEstimate(flops=2*4*KV*CH*rows*wide*HD,bytes_accessed=KV*CH*rows*wide*2+8*rows*8192,transcendentals=0),
        )(e,qt,dott,li,*ks,*vs)


def forward(x, k):
    return lax.ppermute(x, "seq", [(i, i + k) for i in range(8 - k)])


def backward(x, k):
    return lax.ppermute(x, "seq", [(i + k, i) for i in range(8 - k)])


def along_y(x, k):
    return lax.ppermute(x, "dp", [(i, (i + 4 * k) % 16) for i in range(16)])


def flip_dp(x, m):
    return lax.ppermute(x, "dp", [(i, i ^ m) for i in range(16)])


def flip_seq(x, m):
    return lax.ppermute(x, "seq", [(i, i ^ m) for i in range(8)])


def flip_both(x, a, b):
    return lax.ppermute(x, ("dp", "seq"), [(i * 8 + j, (i ^ a) * 8 + (j ^ b)) for i in range(16) for j in range(8)])


def pick(x, i):
    return lax.dynamic_index_in_dim(x, i, 0, keepdims=False)


def place(parts, ids):
    out = jnp.zeros((len(parts),) + parts[0].shape, parts[0].dtype)
    for part, i in zip(parts, ids):
        out = lax.dynamic_update_index_in_dim(out, part, i, 0)
    return out


def body(hidden, weight, query, key, cot, lengths):
    rows = hidden.shape[0]
    dp = lax.axis_index("dp")
    seq = lax.axis_index("seq")
    y, u = dp // 4, dp % 4
    zl, core = u // 2, u % 2
    x, zh = seq // 2, seq % 2
    depth = hidden.shape[1] // 4
    meta = jnp.concatenate([lengths[0], seq.astype(jnp.int32)[None]])
    with jax.named_scope("keys_forward"):
        ks = [forward(key, CH - 1 - c) for c in range(CH - 1)] + [key]
    with jax.named_scope("hidden_columns"):
        blocks = [lax.dynamic_slice_in_dim(hidden, ((y + k) % 4) * depth, depth, axis=1) for k in range(4)]
        hid = jnp.concatenate([blocks[0]] + [along_y(blocks[k], k) for k in (1, 2, 3)], axis=0)
    with jax.named_scope("weight_rows"):
        w1 = flip_dp(weight, 1)
        w2 = flip_dp(weight, 2)
        w3 = flip_dp(w2, 1)
        wu = place([weight, w1, w2, w3], [u, u ^ 1, u ^ 2, u ^ 3]).reshape(depth, -1)
    with jax.named_scope("values"):
        part = jnp.dot(hid, wu, preferred_element_type=f32)
        back = [along_y(part[k * rows : (k + 1) * rows].astype(bf), 4 - k) for k in (1, 2, 3)]
        values = (part[:rows] + sum(b.astype(f32) for b in back)).astype(bf)
        vs = [forward(values, CH - 1 - c) for c in range(CH - 1)] + [values]
    with jax.named_scope("probs"):
        e, qt, dott, li, *dv = probs_call(meta, query, cot, ks)
    with jax.named_scope("value_grad"):
        vgrad = (dv[-1] + sum(backward(dv[c], CH - 1 - c).astype(f32) for c in range(CH - 1))).astype(bf)
        vy = jnp.concatenate([vgrad] + [along_y(vgrad, k) for k in (1, 2, 3)], axis=0)
    with jax.named_scope("weight_grad"):
        g = lax.dot_general(hid, vy, (((0,), (0,)), ((), ())), preferred_element_type=f32)
        g = g.reshape(2, 2, weight.shape[0], -1)
        mine = lax.dynamic_index_in_dim(g, core, 1, keepdims=False)
        other = lax.dynamic_index_in_dim(g, 1 - core, 1, keepdims=False)
        g = mine + flip_dp(other.astype(bf), 1).astype(f32)
        g = g.reshape(2, 2, weight.shape[0] // 2, -1)

        def piece(a, b):
            return pick(pick(g, zl ^ a), zh ^ b)

        g = (
            piece(0, 0)
            + flip_both(piece(1, 0).astype(bf), 2, 0).astype(f32)
            + flip_both(piece(0, 1).astype(bf), 0, 1).astype(f32)
            + flip_both(piece(1, 1).astype(bf), 2, 1).astype(f32)
        )
        g = g.reshape(4, weight.shape[0] // 8, -1)
        g = pick(g, x) + sum(flip_seq(pick(g, x ^ k).astype(bf), 2 * k).astype(f32) for k in (1, 2, 3))
        g = g.astype(bf)
        g = place([g] + [flip_seq(g, 2 * k) for k in (1, 2, 3)], [x, x ^ 1, x ^ 2, x ^ 3])
        wgrad = place([g, flip_seq(g, 1)], [zh, 1 - zh]).reshape(weight.shape).astype(f32)
    with jax.named_scope("input_grad"):
        ig = lax.dot_general(vy, wu, (((1,), (1,)), ((), ())), preferred_element_type=f32).astype(bf)
        igs = [ig[:rows]] + [along_y(ig[k * rows : (k + 1) * rows], 4 - k) for k in (1, 2, 3)]
        input_grad = jnp.zeros(hidden.shape, bf)
        for k in range(4):
            input_grad = lax.dynamic_update_slice_in_dim(input_grad, igs[k], ((y + k) % 4) * depth, axis=1)
    with jax.named_scope("grads"):
        out, dq, *dk = grads_call(e, qt, dott, li, ks, vs)
    with jax.named_scope("key_grad"):
        kgrad = (dk[-1] + sum(backward(dk[c], CH - 1 - c).astype(f32) for c in range(CH - 1))).astype(bf)
    return out, dq, kgrad, input_grad, wgrad


def solution(mesh):
    tok = P(("dp", "seq"), None)
    own = P("dp", None)
    return jax.shard_map(
        body,
        mesh=mesh,
        in_specs=(tok, own, tok, tok, tok, own),
        out_specs=(tok, tok, tok, tok, own),
        check_vma=False,
    )
```

```python
import functools
import math

import jax
import jax.numpy as jnp
from jax import lax
from jax.experimental import pallas as pl
from jax.experimental.pallas import tpu as pltpu
from jax.sharding import PartitionSpec as P

HD = 128
KV = 8
G = 8
CH = 5
SC = HD**-0.5
L2 = SC * math.log2(math.e)
bf = jnp.bfloat16
f32 = jnp.float32
VL = 56 * 1024 * 1024

def probs_kernel(meta, q, do, k0, k1, k2, k3, k4, *rest):
    e_out, qt_out, dot_out, li_out, v0, v1, v2, v3, v4, bias = rest[-10:]
    rows = q.shape[0]
    @pl.when(pl.program_id(0)==0)
    def _():
        s=meta[KV]
        r=lax.broadcasted_iota(jnp.int32,(1,rows),1)
        pos=r+s*rows
        start=jnp.zeros((1,rows),jnp.int32)
        total=meta[0]
        for d in range(1,8):
            start=jnp.where(pos>=total,total,start)
            total=total+meta[d]
        low=start-(s-(CH-1))*rows
        j=lax.broadcasted_iota(jnp.int32,(CH*rows,rows),0)
        ok=(j>=low)&(j<=r+(CH-1)*rows)
        bias[...]=jnp.where(ok,0.0,-1e30)
    for h in range(G):
        qt_out[0,:,h*rows:(h+1)*rows]=q[:,h*HD:(h+1)*HD].T
    ks=(k0,k1,k2,k3,k4)
    W=2
    n=W*rows
    for p in range(G//W):
        cols=slice(p*n,(p+1)*n)
        qt=qt_out[0,:,cols]
        ts=[]
        for c in range(CH):
            b=bias[c*rows:(c+1)*rows,:]
            b=jnp.concatenate([b]*W,axis=1)
            ts.append(jnp.dot(ks[c][...],qt,preferred_element_type=f32)*L2+b)
        m=functools.reduce(jnp.maximum,[jnp.max(t,axis=0,keepdims=True) for t in ts])
        l=jnp.zeros((1,n),f32)
        for c in range(CH):
            e=jnp.exp2(ts[c]-m)
            l=l+jnp.sum(e,axis=0,keepdims=True)
            e_out[0,c*rows:(c+1)*rows,cols]=e.astype(bf)
        li=1.0/l
        li_out[0,:,cols]=jnp.broadcast_to(li,(8,n))
        dt=jnp.concatenate([do[:,h*HD:(h+1)*HD].T for h in range(p*W,(p+1)*W)],axis=1)
        dot_out[0,:,cols]=(dt.astype(f32)*li).astype(bf)
    dall=dot_out[0]
    for c,v in enumerate((v0,v1,v2,v3,v4)):
        v[...]=lax.dot_general(e_out[0,c*rows:(c+1)*rows,:],dall,(((1,),(1,)),((),())),preferred_element_type=f32).astype(v.dtype)

def probs_call(meta, q, do, ks, first, heads, held):
    rows = q.shape[0]
    wide = G * rows
    S = jax.ShapeDtypeStruct

    def narrow():
        return pl.BlockSpec((rows, HD), lambda j: (0, j + first))

    def broad():
        return pl.BlockSpec((rows, G * HD), lambda j: (0, j + first))

    def whole(a, b):
        return pl.BlockSpec((1, a, b), lambda j: (j + first, 0, 0))

    outs = [S((KV, CH * rows, wide), bf), S((KV, HD, wide), bf), S((KV, HD, wide), bf), S((KV, 8, wide), f32)]
    outs += [S((rows, KV * HD), bf)] * (CH - 1) + [S((rows, KV * HD), f32)]
    ins = [pl.BlockSpec(memory_space=pltpu.SMEM), broad(), broad()] + [narrow() for _ in range(CH)]
    return pl.pallas_call(
        probs_kernel,
        grid=(heads,),
        in_specs=ins + [pl.BlockSpec(memory_space=pl.ANY) for _ in held],
        out_specs=[whole(CH * rows, wide), whole(HD, wide), whole(HD, wide), whole(8, wide)] + [narrow() for _ in range(CH)],
        out_shape=outs,
        scratch_shapes=[pltpu.VMEM((CH * rows, rows), f32)],
        input_output_aliases={len(ins) + i: i for i in range(len(held))},
        compiler_params=pltpu.CompilerParams(vmem_limit_bytes=VL),
        cost_estimate=pl.CostEstimate(
            flops=4 * heads * CH * rows * wide * HD,
            bytes_accessed=heads * CH * rows * wide * 2 + heads * rows * 8192,
            transcendentals=heads * CH * rows * wide,
        ),
    )(meta, q, do, *ks, *held)


def grads_kernel(e,qt,dott,li,k0,k1,k2,k3,k4,v0,v1,v2,v3,v4,out,dq,g0,g1,g2,g3,g4,ds):
    rows=out.shape[0]
    ks=(k0,k1,k2,k3,k4); vs=(v0,v1,v2,v3,v4)
    W=2; n=W*rows
    kt=jnp.concatenate([k[...].T for k in ks],axis=1)
    vt=jnp.concatenate([v[...].T for v in vs],axis=1)
    for p in range(G//W):
        cols=slice(p*n,(p+1)*n)
        o=jnp.dot(vt,e[0,:,cols],preferred_element_type=f32)*li[0,0:1,cols]
        ob=o.astype(bf)
        dt=dott[0,:,cols]
        delta=jnp.sum(dt.astype(f32)*o,axis=0,keepdims=True)
        for c in range(CH):
            dp=jnp.dot(vs[c][...],dt,preferred_element_type=f32)
            ds[c*rows:(c+1)*rows,cols]=(e[0,c*rows:(c+1)*rows,cols].astype(f32)*(dp-delta)).astype(bf)
        dqt=(jnp.dot(kt,ds[:,cols],preferred_element_type=f32)*SC).astype(bf)
        for w in range(W):
            h=p*W+w
            out[:,h*HD:(h+1)*HD]=ob[:,w*rows:(w+1)*rows].T
            dq[:,h*HD:(h+1)*HD]=dqt[:,w*rows:(w+1)*rows].T
    qall=qt[0]
    for c,g in enumerate((g0,g1,g2,g3,g4)):
        g[...]=(lax.dot_general(ds[c*rows:(c+1)*rows,:],qall,(((1,),(1,)),((),())),preferred_element_type=f32)*SC).astype(g.dtype)

def grads_call(e,qt,dott,li,ks,vs):
    rows=ks[0].shape[0]; wide=G*rows
    bs=lambda: pl.BlockSpec((rows,HD),lambda j:(0,j))
    bw=lambda: pl.BlockSpec((rows,G*HD),lambda j:(0,j))
    b3=lambda a,b: pl.BlockSpec((1,a,b),lambda j:(j,0,0))
    S=jax.ShapeDtypeStruct
    return pl.pallas_call(grads_kernel,grid=(KV,),
        in_specs=[b3(CH*rows,wide),b3(HD,wide),b3(HD,wide),b3(8,wide)]+[bs() for _ in range(2*CH)],
        out_specs=[bw(),bw()]+[bs() for _ in range(CH)],
        out_shape=[S((rows,KV*G*HD),bf)]*2+[S((rows,KV*HD),bf)]*(CH-1)+[S((rows,KV*HD),f32)],
        scratch_shapes=[pltpu.VMEM((CH*rows,wide),bf)],
        compiler_params=pltpu.CompilerParams(vmem_limit_bytes=VL),
        cost_estimate=pl.CostEstimate(flops=2*4*KV*CH*rows*wide*HD,bytes_accessed=KV*CH*rows*wide*2+8*rows*8192,transcendentals=0),
        )(e,qt,dott,li,*ks,*vs)


def forward(x, k):
    return lax.ppermute(x, ("x", "zh"), [(i, i + k) for i in range(8 - k)])


def backward(x, k):
    return lax.ppermute(x, ("x", "zh"), [(i + k, i) for i in range(8 - k)])


def flip(x, axis):
    return lax.ppermute(x, axis, [(0, 1), (1, 0)])


def along_y(x, k):
    return lax.ppermute(x, "y", [(i, (i + k) % 4) for i in range(4)])


def ordered(own, other, index, axis):
    first = index == 0
    return jnp.stack([jnp.where(first, own, other), jnp.where(first, other, own)], axis=axis)


def body(hidden, weight, query, key, cot, lengths):
    rows = hidden.shape[0]
    high, width = weight.shape
    y, zl, core = (lax.axis_index(n) for n in ("y", "zl", "core"))
    seq = lax.axis_index(("x", "zh"))
    depth = hidden.shape[1] // 4
    meta = jnp.concatenate([lengths[0], seq.astype(jnp.int32)[None]])
    with jax.named_scope("keys_forward"):
        ks = [forward(key, CH - 1 - c) for c in range(CH - 1)] + [key]
    with jax.named_scope("hidden_columns"):
        hid = lax.all_to_all(hidden.reshape(rows, 4, depth), "y", 1, 0, tiled=True).reshape(4 * rows, depth)
    with jax.named_scope("weight_rows"):
        wz = ordered(weight, flip(weight, "zl"), zl, 0)
        wz, ks, hid = lax.optimization_barrier((wz, ks, hid))
        wu = ordered(wz, flip(wz, "core"), core, 1).reshape(depth, width)
    with jax.named_scope("probs"):
        held = probs_call(meta, query, cot, ks, 0, KV // 2, [])
    with jax.named_scope("values"):
        part = jnp.dot(hid, wu, preferred_element_type=f32).astype(bf).reshape(4, rows, width)
        part, held = lax.optimization_barrier((part, held))
        part = lax.all_to_all(part, "y", 0, 0, tiled=True)
        values = jnp.sum(part.astype(f32), axis=0).astype(bf)
    with jax.named_scope("probs"):
        e, qt, dott, li, *dv = probs_call(meta, query, cot, ks, KV // 2, KV // 2, held)
    with jax.named_scope("values_forward"):
        vs = [forward(values, CH - 1 - c) for c in range(CH - 1)] + [values]
    with jax.named_scope("value_grad"):
        dv = [backward(dv[c], CH - 1 - c) for c in range(CH - 1)] + [dv[-1]]
        dv, vs[2], vs[3] = lax.optimization_barrier((dv, vs[2], vs[3]))
        vgrad = sum(d.astype(f32) for d in dv).astype(bf)
        vy = jnp.broadcast_to(vgrad[None], (4,) + vgrad.shape)
        vy = lax.all_to_all(vy, "y", 0, 0, tiled=True).reshape(4 * rows, width)
        vy, vs[0], vs[1] = lax.optimization_barrier((vy, vs[0], vs[1]))
    with jax.named_scope("weight_grad"):
        g = lax.dot_general(hid, vy, (((0,), (0,)), ((), ())), preferred_element_type=f32).astype(bf)

        def half(c):
            return jnp.concatenate([lax.dynamic_slice_in_dim(g, (2 * i + c) * high, high) for i in range(2)])

        g = half(core).astype(f32) + flip(half(1 - core), "core").astype(f32)
        g = g.astype(bf).reshape(16, high // 8, width)
    with jax.named_scope("input_grad"):
        ig = lax.dot_general(vy, wu, (((1,), (1,)), ((), ())), preferred_element_type=f32).astype(bf)
    g, ig, vs = lax.optimization_barrier((g, ig, vs))
    with jax.named_scope("grads"):
        out, dq, *dk = grads_call(e, qt, dott, li, ks, vs)
    with jax.named_scope("input_grad"):
        blocks = [lax.dynamic_slice_in_dim(ig, (y - k) % 4 * rows, rows) for k in range(4)]
        igs = [blocks[0]] + [along_y(blocks[k], 4 - k) for k in (1, 2, 3)]
    with jax.named_scope("weight_grad"):
        g = lax.all_to_all(g, ("zl", "x", "zh"), 0, 0, tiled=True)
        g = jnp.sum(g.astype(f32), axis=0).astype(bf)
    g, igs, dk = lax.optimization_barrier((g, igs, dk))
    with jax.named_scope("key_grad"):
        kgrad = (dk[-1] + sum(backward(dk[c], CH - 1 - c).astype(f32) for c in range(CH - 1))).astype(bf)
    with jax.named_scope("weight_grad"):
        g = jnp.broadcast_to(g[None], (8,) + g.shape)
        wgrad = lax.all_to_all(g, ("x", "zh"), 0, 0, tiled=True).reshape(weight.shape).astype(f32)
    with jax.named_scope("input_grad"):
        input_grad = jnp.zeros(hidden.shape, bf)
        for k in range(4):
            input_grad = lax.dynamic_update_slice_in_dim(input_grad, igs[k], (y + k) % 4 * depth, axis=1)
    return out, dq, kgrad, input_grad, wgrad


def solution(mesh):
    fine = jax.sharding.Mesh(mesh.devices.reshape(4, 2, 2, 4, 2), ("y", "zl", "core", "x", "zh"))
    tok = P(("y", "zl", "core", "x", "zh"), None)
    own = P(("y", "zl", "core"), None)
    return jax.shard_map(
        body,
        mesh=fine,
        in_specs=(tok, own, tok, tok, tok, own),
        out_specs=(tok, tok, tok, tok, own),
        check_vma=False,
    )
```

```python
import functools
import math

import jax
import jax.numpy as jnp
from jax import lax
from jax.experimental import pallas as pl
from jax.experimental.pallas import tpu as pltpu
from jax.sharding import PartitionSpec as P

HD = 128
KV = 8
G = 8
CH = 5
N = 8
SC = HD**-0.5
L2 = SC * math.log2(math.e)
bf = jnp.bfloat16
f32 = jnp.float32
VL = 56 * 1024 * 1024
W = 4
FAR = 2
RB = 128
HP = 2


def key_mask(meta, rows, first, chunks):
    s = meta[KV]
    r = lax.broadcasted_iota(jnp.int32, (1, rows), 1)
    pos = r + s * rows
    start = jnp.zeros((1, rows), jnp.int32)
    total = meta[0]
    for d in range(1, KV):
        start = jnp.where(pos >= total, total, start)
        total = total + meta[d]
    low = start - (s - (CH - 1)) * rows
    j = lax.broadcasted_iota(jnp.int32, (chunks * rows, rows), 0) + first * rows
    return jnp.where((j >= low) & (j <= r + (CH - 1) * rows), 0.0, -1e30)


def exponentials(ks, qt, bias, e_out, cols):
    rows = bias.shape[1]
    ts = []
    for c, k in enumerate(ks):
        b = jnp.concatenate([bias[c * rows : (c + 1) * rows, :]] * W, axis=1)
        ts.append(jnp.dot(k[...], qt, preferred_element_type=f32) * L2 + b)
    m = functools.reduce(jnp.maximum, [jnp.max(t, axis=0, keepdims=True) for t in ts])
    l = jnp.zeros_like(m)
    for c, t in enumerate(ts):
        e = jnp.exp2(t - m)
        l = l + jnp.sum(e, axis=0, keepdims=True)
        e_out[0, c * rows : (c + 1) * rows, cols] = e.astype(bf)
    return m, l


def near_kernel(meta, q, do, k2, k3, k4, e_out, qt_out, dt_out, stat, bias):
    rows = q.shape[0]

    @pl.when(pl.program_id(0) == 0)
    def _():
        bias[...] = key_mask(meta, rows, FAR, CH - FAR)

    n = W * rows
    for p in range(G // W):
        cols = slice(p * n, (p + 1) * n)
        for h in range(p * W, (p + 1) * W):
            qt_out[0, :, h * rows : (h + 1) * rows] = q[:, h * HD : (h + 1) * HD].T
            dt_out[0, :, h * rows : (h + 1) * rows] = do[:, h * HD : (h + 1) * HD].T
        m, l = exponentials((k2, k3, k4), qt_out[0, :, cols], bias, e_out, cols)
        stat[0, 0:1, cols] = m
        stat[0, 1:2, cols] = l


def far_kernel(meta, qt, dt, e1, stat, k01, e_out, a_out, v01, v2, v3, v4, bias, d1, d2):
    rows = v2.shape[0]

    @pl.when(pl.program_id(0) == 0)
    def _():
        bias[...] = key_mask(meta, rows, 0, FAR)

    n = W * rows
    for p in range(G // W):
        cols = slice(p * n, (p + 1) * n)
        m2, l2 = exponentials((k01.at[0], k01.at[1]), qt[0, :, cols], bias, e_out, cols)
        m1, l1 = stat[0, 0:1, cols], stat[0, 1:2, cols]
        m = jnp.maximum(m1, m2)
        w1, w2 = jnp.exp2(m1 - m), jnp.exp2(m2 - m)
        inv = 1.0 / (l1 * w1 + l2 * w2)
        a1, a2 = w1 * inv, w2 * inv
        a_out[0, 0:1, cols] = a1
        a_out[0, 1:2, cols] = a2
        d = dt[0, :, cols].astype(f32)
        d1[:, cols] = (d * a1).astype(bf)
        d2[:, cols] = (d * a2).astype(bf)
    nt = (((1,), (1,)), ((), ()))
    for c, v in enumerate((v01.at[0], v01.at[1], v2, v3, v4)):
        if c < FAR:
            e, d = e_out[0, c * rows : (c + 1) * rows, :], d2[...]
        else:
            e, d = e1[0, (c - FAR) * rows : (c - FAR + 1) * rows, :], d1[...]
        v[...] = lax.dot_general(e, d, nt, preferred_element_type=f32).astype(v.dtype)


def grads_kernel(qt, dt, e1, e2, a, k01, k2, k3, k4, v01, v2, v3, v4, out, dq, g0, g1, g2, g3, g4, ds):
    rows = out.shape[0]
    ks = (k01.at[0], k01.at[1], k2, k3, k4)
    vs = (v01.at[0], v01.at[1], v2, v3, v4)
    n = W * rows
    kt = jnp.concatenate([k[...].T for k in ks], axis=1)
    vt1 = jnp.concatenate([v[...].T for v in vs[FAR:]], axis=1)
    vt2 = jnp.concatenate([v[...].T for v in vs[:FAR]], axis=1)
    for p in range(G // W):
        cols = slice(p * n, (p + 1) * n)
        a1, a2 = a[0, 0:1, cols], a[0, 1:2, cols]
        o = jnp.dot(vt1, e1[0, :, cols], preferred_element_type=f32) * a1
        o = o + jnp.dot(vt2, e2[0, :, cols], preferred_element_type=f32) * a2
        ob = o.astype(bf)
        d = dt[0, :, cols].astype(f32)
        d1, d2 = (d * a1).astype(bf), (d * a2).astype(bf)
        delta1 = jnp.sum(d1.astype(f32) * o, axis=0, keepdims=True)
        delta2 = jnp.sum(d2.astype(f32) * o, axis=0, keepdims=True)
        for c in range(CH):
            if c < FAR:
                dd, delta, e = d2, delta2, e2[0, c * rows : (c + 1) * rows, cols]
            else:
                dd, delta, e = d1, delta1, e1[0, (c - FAR) * rows : (c - FAR + 1) * rows, cols]
            dp = jnp.dot(vs[c][...], dd, preferred_element_type=f32)
            ds[c * rows : (c + 1) * rows, cols] = (e.astype(f32) * (dp - delta)).astype(bf)
        dqt = (jnp.dot(kt, ds[:, cols], preferred_element_type=f32) * SC).astype(bf)
        for w in range(W):
            h = p * W + w
            out[:, h * HD : (h + 1) * HD] = ob[:, w * rows : (w + 1) * rows].T
            dq[:, h * HD : (h + 1) * HD] = dqt[:, w * rows : (w + 1) * rows].T
    qall = qt[0]
    for c, g in enumerate((g0, g1, g2, g3, g4)):
        dk = lax.dot_general(
            ds[c * rows : (c + 1) * rows, :], qall, (((1,), (1,)), ((), ())), preferred_element_type=f32
        )
        g[...] = (dk * SC).astype(g.dtype)


def view(ref, kind, h):
    if kind == "m":
        return ref
    if kind == "p":
        return ref.at[:, :, pl.ds(h * HD, HD)]
    if kind in ("n", "o"):
        return ref.at[:, pl.ds(h * HD, HD)]
    if kind == "b":
        return ref.at[:, pl.ds(h * G * HD, G * HD)]
    return ref.at[pl.ds(h, 1)]


def call(kernel, args, ins, outs, scratch, products, exps):
    rows = RB
    wide = G * rows
    kinds = ins + outs
    dtypes = {"e1": ((KV, (CH - FAR) * rows, wide), bf), "e2": ((KV, FAR * rows, wide), bf), "t": ((KV, HD, wide), bf)}
    dtypes |= {"s": ((KV, 8, wide), f32), "b": ((rows, KV * G * HD), bf), "n": ((rows, KV * HD), bf)}
    dtypes |= {"o": ((rows, KV * HD), f32), "p": ((FAR, rows, KV * HD), bf)}

    def spec(kind):
        if kind == "m":
            return pl.BlockSpec(memory_space=pltpu.SMEM)
        if kind == "p":
            return pl.BlockSpec((FAR, rows, HP * HD), lambda j: (0, 0, j))
        if kind in ("n", "o"):
            return pl.BlockSpec((rows, HP * HD), lambda j: (0, j))
        if kind == "b":
            return pl.BlockSpec((rows, HP * G * HD), lambda j: (0, j))
        return pl.BlockSpec((HP,) + dtypes[kind][0][1:], lambda j: (j, 0, 0))

    def heads(*refs):
        for h in range(HP):
            kernel(*[view(r, k, h) for r, k in zip(refs, kinds)], *refs[len(kinds) :])

    return pl.pallas_call(
        heads,
        grid=(KV // HP,),
        in_specs=[spec(k) for k in ins],
        out_specs=[spec(k) for k in outs],
        out_shape=[jax.ShapeDtypeStruct(*dtypes[k]) for k in outs],
        scratch_shapes=scratch,
        compiler_params=pltpu.CompilerParams(vmem_limit_bytes=VL),
        cost_estimate=pl.CostEstimate(
            flops=products * 2 * KV * rows * wide * HD, bytes_accessed=16 << 20, transcendentals=exps * KV * rows * wide
        ),
    )(*args)


def near_call(meta, q, do, ks):
    scratch = [pltpu.VMEM(((CH - FAR) * RB, RB), f32)]
    ins = ["m", "b", "b"] + ["n"] * (CH - FAR)
    return call(near_kernel, (meta, q, do, *ks), ins, ["e1", "t", "t", "s"], scratch, CH - FAR, CH - FAR)


def far_call(meta, near, ks):
    e1, qt, dt, stat = near
    scratch = [pltpu.VMEM((FAR * RB, RB), f32)] + [pltpu.VMEM((HD, G * RB), bf)] * 2
    ins = ["m", "t", "t", "e1", "s", "p"]
    outs = ["e2", "s", "p", "n", "n", "o"]
    return call(far_kernel, (meta, qt, dt, e1, stat, ks), ins, outs, scratch, FAR + CH, FAR)


def grads_call(near, e2, a, ks, vs):
    e1, qt, dt, _ = near
    scratch = [pltpu.VMEM((CH * RB, G * RB), bf)]
    ins = ["t", "t", "e1", "e2", "s"] + ["p", "n", "n", "n"] * 2
    outs = ["b", "b"] + ["n"] * (CH - 1) + ["o"]
    return call(grads_kernel, (qt, dt, e1, e2, a, *ks, *vs), ins, outs, scratch, 4 * CH, 0)


def forward(x, k):
    return lax.ppermute(x, ("x", "zh"), [(i, i + k) for i in range(N - k)])


def backward(x, k):
    return lax.ppermute(x, ("x", "zh"), [(i + k, i) for i in range(N - k)])


def flip(x, axis):
    return lax.ppermute(x, axis, [(0, 1), (1, 0)])


def along_y(x, k):
    return lax.ppermute(x, "y", [(i, (i + k) % 4) for i in range(4)])


def over_seq(x):
    return lax.all_to_all(x, ("x", "zh"), 0, 0, tiled=True)


def ordered(own, other, index, axis):
    first = index == 0
    return jnp.stack([jnp.where(first, own, other), jnp.where(first, other, own)], axis=axis)


def relay_sum(parts, got):
    _, two, one, own = parts
    two = (two.astype(f32) + got[0].astype(f32)).astype(bf)
    one = (one.astype(f32) + got[1].astype(f32)).astype(bf)
    return own, backward(two, 2), backward(one, 1)


def turned(x, start, rows):
    n = x.shape[0] // rows
    return jnp.concatenate([lax.dynamic_slice_in_dim(x, (start - k) % n * rows, rows) for k in range(n)])


def body(hidden, weight, query, key, cot, lengths):
    rows = hidden.shape[0]
    high, width = weight.shape
    y, zl, core = (lax.axis_index(n) for n in ("y", "zl", "core"))
    seq = lax.axis_index(("x", "zh"))
    depth = hidden.shape[1] // 4
    meta = jnp.concatenate([lengths[0], seq.astype(jnp.int32)[None]])
    with jax.named_scope("keys"):
        k2, k3 = forward(key, 2), forward(key, 1)
    with jax.named_scope("hidden_columns"):
        hid = lax.all_to_all(hidden.reshape(rows, 4, depth), "y", 1, 0, tiled=True).reshape(4 * rows, depth)
    with jax.named_scope("weight_rows"):
        wz = flip(weight, "zl")
        wz, k2, k3, hid = lax.optimization_barrier((wz, k2, k3, hid))
        wz = ordered(weight, wz, zl, 0)
        wu = ordered(wz, flip(wz, "core"), core, 1).reshape(depth, width)
    with jax.named_scope("keys"):
        k01 = forward(jnp.stack([k2, k3]), 2)
    with jax.named_scope("probs_near"):
        near = near_call(meta, query, cot, (k2, k3, key))
    with jax.named_scope("values"):
        wu, k01 = lax.optimization_barrier((wu, k01))
        part = jnp.dot(hid, wu, preferred_element_type=f32).astype(bf).reshape(4, rows, width)
        part, near = lax.optimization_barrier((part, near))
        part = lax.all_to_all(part, "y", 0, 0, tiled=True)
        values = jnp.sum(part.astype(f32), axis=0).astype(bf)
    with jax.named_scope("probs_far"):
        e2, a, *dv = far_call(meta, near, k01)
    with jax.named_scope("values_forward"):
        v2, v3 = forward(values, 2), forward(values, 1)
        v01 = forward(jnp.stack([v2, v3]), 2)
    with jax.named_scope("value_grad"):
        dv = relay_sum(dv, backward(dv[0], 2))
        dv, v01, v2, v3 = lax.optimization_barrier((dv, v01, v2, v3))
        vgrad = sum(d.astype(f32) for d in dv).astype(bf)
        vys = [vgrad] + [along_y(vgrad, k) for k in (1, 2, 3)]
        vy = jnp.concatenate(vys)
        vs = (v01, v2, v3, values)
    with jax.named_scope("weight_grad"):
        turned_hid = turned(hid, y, rows)
        g = lax.dot_general(turned_hid, vy, (((0,), (0,)), ((), ())), preferred_element_type=f32).astype(bf)

        def half(c):
            return jnp.concatenate([lax.dynamic_slice_in_dim(g, (2 * i + c) * high, high) for i in range(2)])

        g = half(core).astype(f32) + flip(half(1 - core), "core").astype(f32)
        g = g.astype(bf).reshape(2 * N, high // N, width)
    with jax.named_scope("input_grad"):
        ig = lax.dot_general(vy, wu, (((1,), (1,)), ((), ())), preferred_element_type=f32).astype(bf)
        g, ig, vs = lax.optimization_barrier((g, ig, vs))
        igs = [ig[k * rows : (k + 1) * rows] for k in range(4)]
        igs = [igs[0]] + [along_y(igs[k], 4 - k) for k in (1, 2, 3)]
    with jax.named_scope("weight_grad"):
        g = lax.all_to_all(g, ("zl", "x", "zh"), 0, 0, tiled=True)
        g = jnp.sum(g.astype(f32), axis=0).astype(bf)
    with jax.named_scope("grads"):
        out, dq, *dk = grads_call(near, e2, a, (k01, k2, k3, key), vs)
        g, dk, igs = lax.optimization_barrier((g, dk, igs))
    with jax.named_scope("key_grad"):
        dk = [backward(dk[c], CH - 1 - c) for c in range(CH - 1)] + [dk[-1]]
        kgrad = sum(d.astype(f32) for d in dk).astype(bf)
    with jax.named_scope("weight_grad"):
        g = jnp.broadcast_to(g[None], (N,) + g.shape)
        wgrad = over_seq(g).reshape(weight.shape).astype(f32)
    with jax.named_scope("input_grad"):
        input_grad = jnp.zeros(hidden.shape, bf)
        for k in range(4):
            input_grad = lax.dynamic_update_slice_in_dim(input_grad, igs[k], (y + k) % 4 * depth, axis=1)
    return out, dq, kgrad, input_grad, wgrad


def solution(mesh):
    fine = jax.sharding.Mesh(mesh.devices.reshape(4, 2, 2, 4, 2), ("y", "zl", "core", "x", "zh"))
    tok = P(("y", "zl", "core", "x", "zh"), None)
    own = P(("y", "zl", "core"), None)
    return jax.shard_map(
        body,
        mesh=fine,
        in_specs=(tok, own, tok, tok, tok, own),
        out_specs=(tok, tok, tok, tok, own),
        check_vma=False,
    )
```

```python
import functools
import math

import jax
import jax.numpy as jnp
from jax import lax
from jax.experimental import pallas as pl
from jax.experimental.pallas import tpu as pltpu
from jax.sharding import PartitionSpec as P

HD = 128
KV = 8
G = 8
CH = 5
N = 8
SC = HD**-0.5
L2 = SC * math.log2(math.e)
bf = jnp.bfloat16
f32 = jnp.float32
VL = 56 * 1024 * 1024
W = 8
FAR = 2
RB = 128
WP = 4


def probs_kernel(meta, q, do, k01, k2, k3, k4, e_out, qt_out, dt_out, li_out, v01, v2, v3, v4, bias):
    rows = q.shape[0]
    ks = (k01.at[0], k01.at[1], k2, k3, k4)

    @pl.when(pl.program_id(0) == 0)
    def _():
        s = meta[KV]
        r = lax.broadcasted_iota(jnp.int32, (1, rows), 1)
        pos = r + s * rows
        start = jnp.zeros((1, rows), jnp.int32)
        total = meta[0]
        for d in range(1, KV):
            start = jnp.where(pos >= total, total, start)
            total = total + meta[d]
        low = start - (s - (CH - 1)) * rows
        j = lax.broadcasted_iota(jnp.int32, (CH * rows, rows), 0)
        bias[...] = jnp.where((j >= low) & (j <= r + (CH - 1) * rows), 0.0, -1e30)

    n = WP * rows
    for p in range(G // WP):
        cols = slice(p * n, (p + 1) * n)
        for h in range(p * WP, (p + 1) * WP):
            qt_out[0, :, h * rows : (h + 1) * rows] = q[:, h * HD : (h + 1) * HD].T
        qt = qt_out[0, :, cols]
        ts = []
        for c, k in enumerate(ks):
            b = jnp.concatenate([bias[c * rows : (c + 1) * rows, :]] * WP, axis=1)
            ts.append(jnp.dot(k[...], qt, preferred_element_type=f32) * L2 + b)
        m = functools.reduce(jnp.maximum, [jnp.max(t, axis=0, keepdims=True) for t in ts])
        l = jnp.zeros_like(m)
        for c, t in enumerate(ts):
            e = jnp.exp2(t - m)
            l = l + jnp.sum(e, axis=0, keepdims=True)
            e_out[0, c * rows : (c + 1) * rows, cols] = e.astype(bf)
        li = 1.0 / l
        li_out[0, 0:1, cols] = li
        dt = jnp.concatenate([do[:, h * HD : (h + 1) * HD].T for h in range(p * WP, (p + 1) * WP)], axis=1)
        dt_out[0, :, cols] = (dt.astype(f32) * li).astype(bf)
    dall = dt_out[0]
    nt = (((1,), (1,)), ((), ()))
    for c, v in enumerate((v01.at[0], v01.at[1], v2, v3, v4)):
        e = e_out[0, c * rows : (c + 1) * rows, :]
        v[...] = lax.dot_general(e, dall, nt, preferred_element_type=f32).astype(v.dtype)


def grads_kernel(qt, dt, e, li, k01, k2, k3, k4, v01, v2, v3, v4, out, dq, g0, g1, g2, g3, g4, ds):
    rows = out.shape[0]
    ks = (k01.at[0], k01.at[1], k2, k3, k4)
    vs = (v01.at[0], v01.at[1], v2, v3, v4)
    n = W * rows
    kt = jnp.concatenate([k[...].T for k in ks], axis=1)
    vt = jnp.concatenate([v[...].T for v in vs], axis=1)
    for p in range(G // W):
        cols = slice(p * n, (p + 1) * n)
        o = jnp.dot(vt, e[0, :, cols], preferred_element_type=f32) * li[0, 0:1, cols]
        ob = o.astype(bf)
        d = dt[0, :, cols]
        delta = jnp.sum(d.astype(f32) * o, axis=0, keepdims=True)
        for c in range(CH):
            part = slice(c * rows, (c + 1) * rows)
            dp = jnp.dot(vs[c][...], d, preferred_element_type=f32)
            ds[part, cols] = (e[0, part, cols].astype(f32) * (dp - delta)).astype(bf)
        dqt = (jnp.dot(kt, ds[:, cols], preferred_element_type=f32) * SC).astype(bf)
        for w in range(W):
            h = p * W + w
            out[:, h * HD : (h + 1) * HD] = ob[:, w * rows : (w + 1) * rows].T
            dq[:, h * HD : (h + 1) * HD] = dqt[:, w * rows : (w + 1) * rows].T
    nt = (((1,), (1,)), ((), ()))
    for c, g in enumerate((g0, g1, g2, g3, g4)):
        dk = lax.dot_general(ds[c * rows : (c + 1) * rows, :], qt[0], nt, preferred_element_type=f32)
        g[...] = (dk * SC).astype(g.dtype)


def view(ref, kind, h):
    if kind == "m":
        return ref
    if kind == "p":
        return ref.at[:, :, pl.ds(h * HD, HD)]
    if kind in ("n", "o"):
        return ref.at[:, pl.ds(h * HD, HD)]
    if kind == "b":
        return ref.at[:, pl.ds(h * G * HD, G * HD)]
    return ref.at[pl.ds(h, 1)]


def call(kernel, args, ins, outs, scratch, products, exps, hp):
    rows = RB
    wide = G * rows
    kinds = ins + outs
    dtypes = {"e": ((KV, CH * rows, wide), bf), "t": ((KV, HD, wide), bf)}
    dtypes |= {"s": ((KV, 8, wide), f32), "b": ((rows, KV * G * HD), bf), "n": ((rows, KV * HD), bf)}
    dtypes |= {"o": ((rows, KV * HD), f32), "p": ((FAR, rows, KV * HD), bf)}

    def spec(kind):
        if kind == "m":
            return pl.BlockSpec(memory_space=pltpu.SMEM)
        if kind == "p":
            return pl.BlockSpec((FAR, rows, hp * HD), lambda j: (0, 0, j))
        if kind in ("n", "o"):
            return pl.BlockSpec((rows, hp * HD), lambda j: (0, j))
        if kind == "b":
            return pl.BlockSpec((rows, hp * G * HD), lambda j: (0, j))
        return pl.BlockSpec((hp,) + dtypes[kind][0][1:], lambda j: (j, 0, 0))

    def heads(*refs):
        for h in range(hp):
            kernel(*[view(r, k, h) for r, k in zip(refs, kinds)], *refs[len(kinds) :])

    return pl.pallas_call(
        heads,
        grid=(KV // hp,),
        in_specs=[spec(k) for k in ins],
        out_specs=[spec(k) for k in outs],
        out_shape=[jax.ShapeDtypeStruct(*dtypes[k]) for k in outs],
        scratch_shapes=scratch,
        compiler_params=pltpu.CompilerParams(vmem_limit_bytes=VL),
        cost_estimate=pl.CostEstimate(
            flops=products * 2 * KV * rows * wide * HD, bytes_accessed=16 << 20, transcendentals=exps * KV * rows * wide
        ),
    )(*args)


def probs_call(meta, q, do, ks):
    scratch = [pltpu.VMEM((CH * RB, RB), f32)]
    ins = ["m", "b", "b", "p", "n", "n", "n"]
    outs = ["e", "t", "t", "s", "p", "n", "n", "o"]
    return call(probs_kernel, (meta, q, do, *ks), ins, outs, scratch, 2 * CH, CH, 1)


def grads_call(qt, dt, e, li, ks, vs):
    scratch = [pltpu.VMEM((CH * RB, G * RB), bf)]
    ins = ["t", "t", "e", "s"] + ["p", "n", "n", "n"] * 2
    outs = ["b", "b"] + ["n"] * (CH - 1) + ["o"]
    return call(grads_kernel, (qt, dt, e, li, *ks, *vs), ins, outs, scratch, 4 * CH, 0, 2)


def forward(x, k):
    return lax.ppermute(x, ("x", "zh"), [(i, i + k) for i in range(N - k)])


def backward(x, k):
    return lax.ppermute(x, ("x", "zh"), [(i + k, i) for i in range(N - k)])


def flip(x, axis):
    return lax.ppermute(x, axis, [(0, 1), (1, 0)])


def along_y(x, k):
    return lax.ppermute(x, "y", [(i, (i + k) % 4) for i in range(4)])


def over_seq(x):
    return lax.all_to_all(x, ("x", "zh"), 0, 0, tiled=True)


def ordered(own, other, index, axis):
    first = index == 0
    return jnp.stack([jnp.where(first, own, other), jnp.where(first, other, own)], axis=axis)


def relay_sum(parts, got):
    _, two, one, own = parts
    two = (two.astype(f32) + got[0].astype(f32)).astype(bf)
    one = (one.astype(f32) + got[1].astype(f32)).astype(bf)
    return own, backward(two, 2), backward(one, 1)


def turned(x, start, rows):
    n = x.shape[0] // rows
    return jnp.concatenate([lax.dynamic_slice_in_dim(x, (start - k) % n * rows, rows) for k in range(n)])


def body(hidden, weight, query, key, cot, lengths):
    rows = hidden.shape[0]
    high, width = weight.shape
    y, zl, core = (lax.axis_index(n) for n in ("y", "zl", "core"))
    seq = lax.axis_index(("x", "zh"))
    depth = hidden.shape[1] // 4
    meta = jnp.concatenate([lengths[0], seq.astype(jnp.int32)[None]])
    with jax.named_scope("keys"):
        k2, k3 = forward(key, 2), forward(key, 1)
    with jax.named_scope("hidden_columns"):
        hid = lax.all_to_all(hidden.reshape(rows, 4, depth), "y", 1, 0, tiled=True).reshape(4 * rows, depth)
    with jax.named_scope("weight_rows"):
        wz = flip(weight, "zl")
        wz, k2, k3, hid = lax.optimization_barrier((wz, k2, k3, hid))
        wz = ordered(weight, wz, zl, 0)
        wu = ordered(wz, flip(wz, "core"), core, 1).reshape(depth, width)
    with jax.named_scope("keys"):
        k01 = forward(jnp.stack([k2, k3]), 2)
    with jax.named_scope("values"):
        part = jnp.dot(hid, wu, preferred_element_type=f32).astype(bf).reshape(4, rows, width)
        part, k2 = lax.optimization_barrier((part, k2))
        part = lax.all_to_all(part, "y", 0, 0, tiled=True)
        values = jnp.sum(part.astype(f32), axis=0).astype(bf)
    with jax.named_scope("probs"):
        e, qt, dt, li, *dv = probs_call(meta, query, cot, (k01, k2, k3, key))
    with jax.named_scope("values_forward"):
        v2, v3 = forward(values, 2), forward(values, 1)
        v01 = forward(jnp.stack([v2, v3]), 2)
    with jax.named_scope("value_grad"):
        dv = relay_sum(dv, backward(dv[0], 2))
        dv, v01, v2, v3 = lax.optimization_barrier((dv, v01, v2, v3))
        vgrad = sum(d.astype(f32) for d in dv).astype(bf)
        vys = [vgrad] + [along_y(vgrad, k) for k in (1, 2, 3)]
        vy = jnp.concatenate(vys)
        vs = (v01, v2, v3, values)
    with jax.named_scope("weight_grad"):
        turned_hid = turned(hid, y, rows)
        g = lax.dot_general(turned_hid, vy, (((0,), (0,)), ((), ())), preferred_element_type=f32).astype(bf)

        def half(c):
            return jnp.concatenate([lax.dynamic_slice_in_dim(g, (2 * i + c) * high, high) for i in range(2)])

        g = half(core).astype(f32) + flip(half(1 - core), "core").astype(f32)
        g = g.astype(bf).reshape(2 * N, high // N, width)
    with jax.named_scope("input_grad"):
        ig = lax.dot_general(vy, wu, (((1,), (1,)), ((), ())), preferred_element_type=f32).astype(bf)
        g, ig, vs = lax.optimization_barrier((g, ig, vs))
        igs = [ig[k * rows : (k + 1) * rows] for k in range(4)]
        igs = [igs[0]] + [along_y(igs[k], 4 - k) for k in (1, 2, 3)]
    with jax.named_scope("weight_grad"):
        g = lax.all_to_all(g, ("zl", "x", "zh"), 0, 0, tiled=True)
        g = jnp.sum(g.astype(f32), axis=0).astype(bf)
    with jax.named_scope("grads"):
        out, dq, *dk = grads_call(qt, dt, e, li, (k01, k2, k3, key), vs)
        g, dk, igs = lax.optimization_barrier((g, dk, igs))
    with jax.named_scope("key_grad"):
        dk = [backward(dk[c], CH - 1 - c) for c in range(CH - 1)] + [dk[-1]]
        kgrad = sum(d.astype(f32) for d in dk).astype(bf)
    with jax.named_scope("weight_grad"):
        g = jnp.broadcast_to(g[None], (N,) + g.shape)
        wgrad = over_seq(g).reshape(weight.shape).astype(f32)
    with jax.named_scope("input_grad"):
        input_grad = jnp.zeros(hidden.shape, bf)
        for k in range(4):
            input_grad = lax.dynamic_update_slice_in_dim(input_grad, igs[k], (y + k) % 4 * depth, axis=1)
    return out, dq, kgrad, input_grad, wgrad


def solution(mesh):
    fine = jax.sharding.Mesh(mesh.devices.reshape(4, 2, 2, 4, 2), ("y", "zl", "core", "x", "zh"))
    tok = P(("y", "zl", "core", "x", "zh"), None)
    own = P(("y", "zl", "core"), None)
    return jax.shard_map(
        body,
        mesh=fine,
        in_specs=(tok, own, tok, tok, tok, own),
        out_specs=(tok, tok, tok, tok, own),
        check_vma=False,
    )
```

```python
import functools
import math

import jax
import jax.numpy as jnp
from jax import lax
from jax.experimental import pallas as pl
from jax.experimental.pallas import tpu as pltpu
from jax.sharding import PartitionSpec as P

HD = 128
KV = 8
G = 8
CH = 5
N = 8
SC = HD**-0.5
L2 = SC * math.log2(math.e)
bf = jnp.bfloat16
f32 = jnp.float32
VL = 56 * 1024 * 1024
W = 8
FAR = 2
RB = 128
WP = 4


def probs_kernel(meta, q, do, k01, k2, k3, k4, e_out, qt_out, dt_out, li_out, v0, v1, v2, v3, v4, bias):
    rows = q.shape[0]
    ks = (k01.at[0], k01.at[1], k2, k3, k4)

    @pl.when(pl.program_id(0) == 0)
    def _():
        s = meta[KV]
        r = lax.broadcasted_iota(jnp.int32, (1, rows), 1)
        pos = r + s * rows
        start = jnp.zeros((1, rows), jnp.int32)
        total = meta[0]
        for d in range(1, KV):
            start = jnp.where(pos >= total, total, start)
            total = total + meta[d]
        low = start - (s - (CH - 1)) * rows
        j = lax.broadcasted_iota(jnp.int32, (CH * rows, rows), 0)
        bias[...] = jnp.where((j >= low) & (j <= r + (CH - 1) * rows), 0.0, -1e30)

    n = WP * rows
    for p in range(G // WP):
        cols = slice(p * n, (p + 1) * n)
        for h in range(p * WP, (p + 1) * WP):
            qt_out[0, :, h * rows : (h + 1) * rows] = q[:, h * HD : (h + 1) * HD].T
        qt = qt_out[0, :, cols]
        ts = []
        for c, k in enumerate(ks):
            b = jnp.concatenate([bias[c * rows : (c + 1) * rows, :]] * WP, axis=1)
            ts.append(jnp.dot(k[...], qt, preferred_element_type=f32) * L2 + b)
        m = functools.reduce(jnp.maximum, [jnp.max(t, axis=0, keepdims=True) for t in ts])
        l = jnp.zeros_like(m)
        for c, t in enumerate(ts):
            e = jnp.exp2(t - m)
            l = l + jnp.sum(e, axis=0, keepdims=True)
            e_out[0, c * rows : (c + 1) * rows, cols] = e.astype(bf)
        li = 1.0 / l
        li_out[0, 0:1, cols] = li
        dt = jnp.concatenate([do[:, h * HD : (h + 1) * HD].T for h in range(p * WP, (p + 1) * WP)], axis=1)
        dt_out[0, :, cols] = (dt.astype(f32) * li).astype(bf)
    dall = dt_out[0]
    nt = (((1,), (1,)), ((), ()))
    for c, v in enumerate((v0, v1, v2, v3, v4)):
        e = e_out[0, c * rows : (c + 1) * rows, :]
        v[...] = lax.dot_general(e, dall, nt, preferred_element_type=f32).astype(v.dtype)


def grads_kernel(qt, dt, e, li, k01, k2, k3, k4, v01, v2, v3, v4, out, dq, g0, g1, g2, g3, g4, ds):
    rows = out.shape[0]
    ks = (k01.at[0], k01.at[1], k2, k3, k4)
    vs = (v01.at[0], v01.at[1], v2, v3, v4)
    n = W * rows
    kt = jnp.concatenate([k[...].T for k in ks], axis=1)
    vt = jnp.concatenate([v[...].T for v in vs], axis=1)
    for p in range(G // W):
        cols = slice(p * n, (p + 1) * n)
        o = jnp.dot(vt, e[0, :, cols], preferred_element_type=f32) * li[0, 0:1, cols]
        ob = o.astype(bf)
        d = dt[0, :, cols]
        delta = jnp.sum(d.astype(f32) * o, axis=0, keepdims=True)
        for c in range(CH):
            part = slice(c * rows, (c + 1) * rows)
            dp = jnp.dot(vs[c][...], d, preferred_element_type=f32)
            ds[part, cols] = (e[0, part, cols].astype(f32) * (dp - delta)).astype(bf)
        dqt = (jnp.dot(kt, ds[:, cols], preferred_element_type=f32) * SC).astype(bf)
        for w in range(W):
            h = p * W + w
            out[:, h * HD : (h + 1) * HD] = ob[:, w * rows : (w + 1) * rows].T
            dq[:, h * HD : (h + 1) * HD] = dqt[:, w * rows : (w + 1) * rows].T
    nt = (((1,), (1,)), ((), ()))
    for c, g in enumerate((g0, g1, g2, g3, g4)):
        dk = lax.dot_general(ds[c * rows : (c + 1) * rows, :], qt[0], nt, preferred_element_type=f32)
        g[...] = (dk * SC).astype(g.dtype)


def view(ref, kind, h):
    if kind == "m":
        return ref
    if kind == "p":
        return ref.at[:, :, pl.ds(h * HD, HD)]
    if kind in ("n", "o"):
        return ref.at[:, pl.ds(h * HD, HD)]
    if kind == "b":
        return ref.at[:, pl.ds(h * G * HD, G * HD)]
    return ref.at[pl.ds(h, 1)]


def call(kernel, args, ins, outs, scratch, products, exps, hp):
    rows = RB
    wide = G * rows
    kinds = ins + outs
    dtypes = {"e": ((KV, CH * rows, wide), bf), "t": ((KV, HD, wide), bf)}
    dtypes |= {"s": ((KV, 8, wide), f32), "b": ((rows, KV * G * HD), bf), "n": ((rows, KV * HD), bf)}
    dtypes |= {"o": ((rows, KV * HD), f32), "p": ((FAR, rows, KV * HD), bf)}

    def spec(kind):
        if kind == "m":
            return pl.BlockSpec(memory_space=pltpu.SMEM)
        if kind == "p":
            return pl.BlockSpec((FAR, rows, hp * HD), lambda j: (0, 0, j))
        if kind in ("n", "o"):
            return pl.BlockSpec((rows, hp * HD), lambda j: (0, j))
        if kind == "b":
            return pl.BlockSpec((rows, hp * G * HD), lambda j: (0, j))
        return pl.BlockSpec((hp,) + dtypes[kind][0][1:], lambda j: (j, 0, 0))

    def heads(*refs):
        for h in range(hp):
            kernel(*[view(r, k, h) for r, k in zip(refs, kinds)], *refs[len(kinds) :])

    return pl.pallas_call(
        heads,
        grid=(KV // hp,),
        in_specs=[spec(k) for k in ins],
        out_specs=[spec(k) for k in outs],
        out_shape=[jax.ShapeDtypeStruct(*dtypes[k]) for k in outs],
        scratch_shapes=scratch,
        compiler_params=pltpu.CompilerParams(vmem_limit_bytes=VL),
        cost_estimate=pl.CostEstimate(
            flops=products * 2 * KV * rows * wide * HD, bytes_accessed=16 << 20, transcendentals=exps * KV * rows * wide
        ),
    )(*args)


def probs_call(meta, q, do, ks):
    scratch = [pltpu.VMEM((CH * RB, RB), f32)]
    ins = ["m", "b", "b", "p", "n", "n", "n"]
    outs = ["e", "t", "t", "s"] + ["n"] * (CH - 1) + ["o"]
    return call(probs_kernel, (meta, q, do, *ks), ins, outs, scratch, 2 * CH, CH, 1)


def grads_call(qt, dt, e, li, ks, vs):
    scratch = [pltpu.VMEM((CH * RB, G * RB), bf)]
    ins = ["t", "t", "e", "s"] + ["p", "n", "n", "n"] * 2
    outs = ["b", "b"] + ["n"] * (CH - 1) + ["o"]
    return call(grads_kernel, (qt, dt, e, li, *ks, *vs), ins, outs, scratch, 4 * CH, 0, 2)


def forward(x, k):
    return lax.ppermute(x, ("x", "zh"), [(i, i + k) for i in range(N - k)])


def backward(x, k):
    return lax.ppermute(x, ("x", "zh"), [(i + k, i) for i in range(N - k)])


def flip(x, axis):
    return lax.ppermute(x, axis, [(0, 1), (1, 0)])


def along_y(x, k):
    return lax.ppermute(x, "y", [(i, (i + k) % 4) for i in range(4)])


def over_seq(x):
    return lax.all_to_all(x, ("x", "zh"), 0, 0, tiled=True)


def ordered(own, other, index, axis):
    first = index == 0
    return jnp.stack([jnp.where(first, own, other), jnp.where(first, other, own)], axis=axis)


def relay_sum(parts, got):
    _, two, one, own = parts
    two = (two.astype(f32) + got[0].astype(f32)).astype(bf)
    one = (one.astype(f32) + got[1].astype(f32)).astype(bf)
    return own, backward(two, 2), backward(one, 1)


def turned(x, start, rows):
    n = x.shape[0] // rows
    return jnp.concatenate([lax.dynamic_slice_in_dim(x, (start - k) % n * rows, rows) for k in range(n)])


def body(hidden, weight, query, key, cot, lengths):
    rows = hidden.shape[0]
    high, width = weight.shape
    y, zl, core = (lax.axis_index(n) for n in ("y", "zl", "core"))
    seq = lax.axis_index(("x", "zh"))
    depth = hidden.shape[1] // 4
    meta = jnp.concatenate([lengths[0], seq.astype(jnp.int32)[None]])
    with jax.named_scope("keys"):
        k2, k3 = forward(key, 2), forward(key, 1)
    with jax.named_scope("hidden_columns"):
        hid = lax.all_to_all(hidden.reshape(rows, 4, depth), "y", 1, 0, tiled=True).reshape(4 * rows, depth)
    with jax.named_scope("weight_rows"):
        wz = flip(weight, "zl")
        wz, k2, k3, hid = lax.optimization_barrier((wz, k2, k3, hid))
        wz = ordered(weight, wz, zl, 0)
        wu = ordered(wz, flip(wz, "core"), core, 1).reshape(depth, width)
    with jax.named_scope("keys"):
        k01 = forward(jnp.stack([k2, k3]), 2)
    with jax.named_scope("values"):
        part = jnp.dot(hid, wu, preferred_element_type=f32).astype(bf).reshape(4, rows, width)
        part, k2 = lax.optimization_barrier((part, k2))
        part = lax.all_to_all(part, "y", 0, 0, tiled=True)
        values = jnp.sum(part.astype(f32), axis=0).astype(bf)
    with jax.named_scope("probs"):
        e, qt, dt, li, *dv = probs_call(meta, query, cot, (k01, k2, k3, key))
    with jax.named_scope("values_forward"):
        v2, v3 = forward(values, 2), forward(values, 1)
    with jax.named_scope("value_grad"):
        dv = [backward(dv[c], CH - 1 - c) for c in range(CH - 1)] + [dv[-1]]
        dv, v2, v3 = lax.optimization_barrier((dv, v2, v3))
        vgrad = sum(d.astype(f32) for d in dv).astype(bf)
        vys = [vgrad] + [along_y(vgrad, k) for k in (1, 2, 3)]
    with jax.named_scope("values_forward"):
        v01 = forward(jnp.stack([v2, v3]), 2)
        vys, v01 = lax.optimization_barrier((vys, v01))
        vy = jnp.concatenate(vys)
        vs = (v01, v2, v3, values)
    with jax.named_scope("weight_grad"):
        turned_hid = turned(hid, y, rows)
        g = lax.dot_general(turned_hid, vy, (((0,), (0,)), ((), ())), preferred_element_type=f32).astype(bf)

        def half(c):
            return jnp.concatenate([lax.dynamic_slice_in_dim(g, (2 * i + c) * high, high) for i in range(2)])

        g = half(core).astype(f32) + flip(half(1 - core), "core").astype(f32)
        g = g.astype(bf).reshape(2 * N, high // N, width)
    with jax.named_scope("input_grad"):
        ig = lax.dot_general(vy, wu, (((1,), (1,)), ((), ())), preferred_element_type=f32).astype(bf)
        g, ig, vs = lax.optimization_barrier((g, ig, vs))
        igs = [ig[k * rows : (k + 1) * rows] for k in range(4)]
        igs = [igs[0]] + [along_y(igs[k], 4 - k) for k in (1, 2, 3)]
    with jax.named_scope("weight_grad"):
        g = lax.all_to_all(g, ("zl", "x", "zh"), 0, 0, tiled=True)
        g = jnp.sum(g.astype(f32), axis=0).astype(bf)
    with jax.named_scope("grads"):
        out, dq, *dk = grads_call(qt, dt, e, li, (k01, k2, k3, key), vs)
        g, dk, igs = lax.optimization_barrier((g, dk, igs))
    with jax.named_scope("key_grad"):
        dk = [backward(dk[c], CH - 1 - c) for c in range(CH - 1)] + [dk[-1]]
        kgrad = sum(d.astype(f32) for d in dk).astype(bf)
    with jax.named_scope("weight_grad"):
        g = jnp.broadcast_to(g[None], (N,) + g.shape)
        wgrad = over_seq(g).reshape(weight.shape).astype(f32)
    with jax.named_scope("input_grad"):
        input_grad = jnp.zeros(hidden.shape, bf)
        for k in range(4):
            input_grad = lax.dynamic_update_slice_in_dim(input_grad, igs[k], (y + k) % 4 * depth, axis=1)
    return out, dq, kgrad, input_grad, wgrad


def solution(mesh):
    fine = jax.sharding.Mesh(mesh.devices.reshape(4, 2, 2, 4, 2), ("y", "zl", "core", "x", "zh"))
    tok = P(("y", "zl", "core", "x", "zh"), None)
    own = P(("y", "zl", "core"), None)
    return jax.shard_map(
        body,
        mesh=fine,
        in_specs=(tok, own, tok, tok, tok, own),
        out_specs=(tok, tok, tok, tok, own),
        check_vma=False,
    )
```

```python
import functools
import math

import jax
import jax.numpy as jnp
from jax import lax
from jax.experimental import pallas as pl
from jax.experimental.pallas import tpu as pltpu
from jax.sharding import PartitionSpec as P

HD = 128
KV = 8
G = 8
CH = 5
N = 8
SC = HD**-0.5
L2 = SC * math.log2(math.e)
bf = jnp.bfloat16
f32 = jnp.float32
VL = 56 * 1024 * 1024
W = 8
FAR = 2
RB = 128
WP = 4


def probs_kernel(meta, q, do, k01, k2, k3, k4, e_out, qt_out, dt_out, li_out, v0, v1, v2, v3, v4, bias):
    rows = q.shape[0]
    ks = (k01.at[0], k01.at[1], k2, k3, k4)

    @pl.when(pl.program_id(0) == 0)
    def _():
        s = meta[KV]
        r = lax.broadcasted_iota(jnp.int32, (1, rows), 1)
        pos = r + s * rows
        start = jnp.zeros((1, rows), jnp.int32)
        total = meta[0]
        for d in range(1, KV):
            start = jnp.where(pos >= total, total, start)
            total = total + meta[d]
        low = start - (s - (CH - 1)) * rows
        j = lax.broadcasted_iota(jnp.int32, (CH * rows, rows), 0)
        bias[...] = jnp.where((j >= low) & (j <= r + (CH - 1) * rows), 0.0, -1e30)

    n = WP * rows
    for p in range(G // WP):
        cols = slice(p * n, (p + 1) * n)
        for h in range(p * WP, (p + 1) * WP):
            qt_out[0, :, h * rows : (h + 1) * rows] = q[:, h * HD : (h + 1) * HD].T
        qt = qt_out[0, :, cols]
        ts = []
        for c, k in enumerate(ks):
            b = jnp.concatenate([bias[c * rows : (c + 1) * rows, :]] * WP, axis=1)
            ts.append(jnp.dot(k[...], qt, preferred_element_type=f32) * L2 + b)
        m = functools.reduce(jnp.maximum, [jnp.max(t, axis=0, keepdims=True) for t in ts])
        l = jnp.zeros_like(m)
        for c, t in enumerate(ts):
            e = jnp.exp2(t - m)
            l = l + jnp.sum(e, axis=0, keepdims=True)
            e_out[0, c * rows : (c + 1) * rows, cols] = e.astype(bf)
        li = 1.0 / l
        li_out[0, 0:1, cols] = li
        dt = jnp.concatenate([do[:, h * HD : (h + 1) * HD].T for h in range(p * WP, (p + 1) * WP)], axis=1)
        dt_out[0, :, cols] = (dt.astype(f32) * li).astype(bf)
    dall = dt_out[0]
    nt = (((1,), (1,)), ((), ()))
    for c, v in enumerate((v0, v1, v2, v3, v4)):
        e = e_out[0, c * rows : (c + 1) * rows, :]
        v[...] = lax.dot_general(e, dall, nt, preferred_element_type=f32).astype(v.dtype)


def grads_kernel(qt, dt, e, li, k01, k2, k3, k4, v01, v2, v3, v4, out, dq, g0, g1, g2, g3, g4, ds):
    rows = out.shape[0]
    ks = (k01.at[0], k01.at[1], k2, k3, k4)
    vs = (v01.at[0], v01.at[1], v2, v3, v4)
    n = W * rows
    kt = jnp.concatenate([k[...].T for k in ks], axis=1)
    vt = jnp.concatenate([v[...].T for v in vs], axis=1)
    for p in range(G // W):
        cols = slice(p * n, (p + 1) * n)
        o = jnp.dot(vt, e[0, :, cols], preferred_element_type=f32) * li[0, 0:1, cols]
        ob = o.astype(bf)
        d = dt[0, :, cols]
        delta = jnp.sum(d.astype(f32) * o, axis=0, keepdims=True)
        for c in range(CH):
            part = slice(c * rows, (c + 1) * rows)
            dp = jnp.dot(vs[c][...], d, preferred_element_type=f32)
            ds[part, cols] = (e[0, part, cols].astype(f32) * (dp - delta)).astype(bf)
        dqt = (jnp.dot(kt, ds[:, cols], preferred_element_type=f32) * SC).astype(bf)
        for w in range(W):
            h = p * W + w
            out[:, h * HD : (h + 1) * HD] = ob[:, w * rows : (w + 1) * rows].T
            dq[:, h * HD : (h + 1) * HD] = dqt[:, w * rows : (w + 1) * rows].T
    nt = (((1,), (1,)), ((), ()))
    for c, g in enumerate((g0, g1, g2, g3, g4)):
        dk = lax.dot_general(ds[c * rows : (c + 1) * rows, :], qt[0], nt, preferred_element_type=f32)
        g[...] = (dk * SC).astype(g.dtype)


def view(ref, kind, h):
    if kind == "m":
        return ref
    if kind == "p":
        return ref.at[:, :, pl.ds(h * HD, HD)]
    if kind in ("n", "o"):
        return ref.at[:, pl.ds(h * HD, HD)]
    if kind == "b":
        return ref.at[:, pl.ds(h * G * HD, G * HD)]
    return ref.at[pl.ds(h, 1)]


def call(kernel, args, ins, outs, scratch, products, exps, hp):
    rows = RB
    wide = G * rows
    kinds = ins + outs
    dtypes = {"e": ((KV, CH * rows, wide), bf), "t": ((KV, HD, wide), bf)}
    dtypes |= {"s": ((KV, 8, wide), f32), "b": ((rows, KV * G * HD), bf), "n": ((rows, KV * HD), bf)}
    dtypes |= {"o": ((rows, KV * HD), f32), "p": ((FAR, rows, KV * HD), bf)}

    def spec(kind):
        if kind == "m":
            return pl.BlockSpec(memory_space=pltpu.SMEM)
        if kind == "p":
            return pl.BlockSpec((FAR, rows, hp * HD), lambda j: (0, 0, j))
        if kind in ("n", "o"):
            return pl.BlockSpec((rows, hp * HD), lambda j: (0, j))
        if kind == "b":
            return pl.BlockSpec((rows, hp * G * HD), lambda j: (0, j))
        return pl.BlockSpec((hp,) + dtypes[kind][0][1:], lambda j: (j, 0, 0))

    def heads(*refs):
        for h in range(hp):
            kernel(*[view(r, k, h) for r, k in zip(refs, kinds)], *refs[len(kinds) :])

    return pl.pallas_call(
        heads,
        grid=(KV // hp,),
        in_specs=[spec(k) for k in ins],
        out_specs=[spec(k) for k in outs],
        out_shape=[jax.ShapeDtypeStruct(*dtypes[k]) for k in outs],
        scratch_shapes=scratch,
        compiler_params=pltpu.CompilerParams(vmem_limit_bytes=VL),
        cost_estimate=pl.CostEstimate(
            flops=products * 2 * KV * rows * wide * HD, bytes_accessed=16 << 20, transcendentals=exps * KV * rows * wide
        ),
    )(*args)


def probs_call(meta, q, do, ks):
    scratch = [pltpu.VMEM((CH * RB, RB), f32)]
    ins = ["m", "b", "b", "p", "n", "n", "n"]
    outs = ["e", "t", "t", "s"] + ["n"] * (CH - 1) + ["o"]
    return call(probs_kernel, (meta, q, do, *ks), ins, outs, scratch, 2 * CH, CH, 1)


def grads_call(qt, dt, e, li, ks, vs):
    scratch = [pltpu.VMEM((CH * RB, G * RB), bf)]
    ins = ["t", "t", "e", "s"] + ["p", "n", "n", "n"] * 2
    outs = ["b", "b"] + ["n"] * (CH - 1) + ["o"]
    return call(grads_kernel, (qt, dt, e, li, *ks, *vs), ins, outs, scratch, 4 * CH, 0, 2)


def forward(x, k):
    return lax.ppermute(x, ("x", "zh"), [(i, i + k) for i in range(N - k)])


def backward(x, k):
    return lax.ppermute(x, ("x", "zh"), [(i + k, i) for i in range(N - k)])


def flip(x, axis):
    return lax.ppermute(x, axis, [(0, 1), (1, 0)])


def along_y(x, k):
    return lax.ppermute(x, "y", [(i, (i + k) % 4) for i in range(4)])


def over_seq(x):
    return lax.all_to_all(x, ("x", "zh"), 0, 0, tiled=True)


def ordered(own, other, index, axis):
    first = index == 0
    return jnp.stack([jnp.where(first, own, other), jnp.where(first, other, own)], axis=axis)


def relay_sum(parts, got):
    _, two, one, own = parts
    two = (two.astype(f32) + got[0].astype(f32)).astype(bf)
    one = (one.astype(f32) + got[1].astype(f32)).astype(bf)
    return own, backward(two, 2), backward(one, 1)


def turned(x, start, rows):
    n = x.shape[0] // rows
    return jnp.concatenate([lax.dynamic_slice_in_dim(x, (start - k) % n * rows, rows) for k in range(n)])


def body(hidden, weight, query, key, cot, lengths):
    rows = hidden.shape[0]
    high, width = weight.shape
    y, zl, core = (lax.axis_index(n) for n in ("y", "zl", "core"))
    seq = lax.axis_index(("x", "zh"))
    depth = hidden.shape[1] // 4
    meta = jnp.concatenate([lengths[0], seq.astype(jnp.int32)[None]])
    with jax.named_scope("keys"):
        k2, k3 = forward(key, 2), forward(key, 1)
    with jax.named_scope("hidden_columns"):
        hid = lax.all_to_all(hidden.reshape(rows, 4, depth), "y", 1, 0, tiled=True).reshape(4 * rows, depth)
    with jax.named_scope("weight_rows"):
        wz = flip(weight, "zl")
        wz, k2, k3, hid = lax.optimization_barrier((wz, k2, k3, hid))
        wz = ordered(weight, wz, zl, 0)
        wu = ordered(wz, flip(wz, "core"), core, 1).reshape(depth, width)
    with jax.named_scope("keys"):
        k01 = forward(jnp.stack([k2, k3]), 2)
    with jax.named_scope("values"):
        part = jnp.dot(hid, wu, preferred_element_type=f32).astype(bf).reshape(4, rows, width)
        part, k2 = lax.optimization_barrier((part, k2))
        part = lax.all_to_all(part, "y", 0, 0, tiled=True)
        values = jnp.sum(part.astype(f32), axis=0).astype(bf)
    with jax.named_scope("probs"):
        e, qt, dt, li, *dv = probs_call(meta, query, cot, (k01, k2, k3, key))
    with jax.named_scope("values_forward"):
        v2, v3 = forward(values, 2), forward(values, 1)
    with jax.named_scope("value_grad"):
        dv = [backward(dv[c], CH - 1 - c) for c in range(CH - 1)] + [dv[-1]]
        dv, v2, v3 = lax.optimization_barrier((dv, v2, v3))
        vgrad = sum(d.astype(f32) for d in dv).astype(bf)
        vys = [vgrad] + [along_y(vgrad, k) for k in (1, 2, 3)]
    with jax.named_scope("values_forward"):
        pair, _ = lax.optimization_barrier(([v2, v3], vgrad))
        v01 = forward(jnp.stack(pair), 2)
        vys, v01 = lax.optimization_barrier((vys, v01))
        vy = jnp.concatenate(vys)
        vs = (v01, v2, v3, values)
    with jax.named_scope("weight_grad"):
        turned_hid = turned(hid, y, rows)
        g = lax.dot_general(turned_hid, vy, (((0,), (0,)), ((), ())), preferred_element_type=f32).astype(bf)

        def half(c):
            return jnp.concatenate([lax.dynamic_slice_in_dim(g, (2 * i + c) * high, high) for i in range(2)])

        g = half(core).astype(f32) + flip(half(1 - core), "core").astype(f32)
        g = g.astype(bf).reshape(2 * N, high // N, width)
    with jax.named_scope("input_grad"):
        ig = lax.dot_general(vy, wu, (((1,), (1,)), ((), ())), preferred_element_type=f32).astype(bf)
        g, ig, vs = lax.optimization_barrier((g, ig, vs))
        igs = [ig[k * rows : (k + 1) * rows] for k in range(4)]
        igs = [igs[0]] + [along_y(igs[k], 4 - k) for k in (1, 2, 3)]
    with jax.named_scope("weight_grad"):
        g = lax.all_to_all(g, ("zl", "x", "zh"), 0, 0, tiled=True)
        g = jnp.sum(g.astype(f32), axis=0).astype(bf)
    with jax.named_scope("grads"):
        out, dq, *dk = grads_call(qt, dt, e, li, (k01, k2, k3, key), vs)
        g, dk, igs = lax.optimization_barrier((g, dk, igs))
    with jax.named_scope("key_grad"):
        dk = [backward(dk[c], CH - 1 - c) for c in range(CH - 1)] + [dk[-1]]
        kgrad = sum(d.astype(f32) for d in dk).astype(bf)
    with jax.named_scope("weight_grad"):
        g = jnp.broadcast_to(g[None], (N,) + g.shape)
        wgrad = over_seq(g).reshape(weight.shape).astype(f32)
    with jax.named_scope("input_grad"):
        input_grad = jnp.zeros(hidden.shape, bf)
        for k in range(4):
            input_grad = lax.dynamic_update_slice_in_dim(input_grad, igs[k], (y + k) % 4 * depth, axis=1)
    return out, dq, kgrad, input_grad, wgrad


def solution(mesh):
    fine = jax.sharding.Mesh(mesh.devices.reshape(4, 2, 2, 4, 2), ("y", "zl", "core", "x", "zh"))
    tok = P(("y", "zl", "core", "x", "zh"), None)
    own = P(("y", "zl", "core"), None)
    return jax.shard_map(
        body,
        mesh=fine,
        in_specs=(tok, own, tok, tok, tok, own),
        out_specs=(tok, tok, tok, tok, own),
        check_vma=False,
    )
```
